32 devices in a mesh: dp: 2 (over y), seq: 4 (over x, core), head: 4 (over z).
Axes of the slice: x: 2, y: 2, z: 4, core: 2. Of those that a mesh axis runs over, the one named last changes fastest.
Arguments:
- target: bfloat16 [4, 1024, 768], P('dp', 'seq'), may hold values from -6 to 6
- memory: bfloat16 [4, 6144, 768], P('dp', 'seq'), may hold values from -6 to 6
- memory_mark: int32 [4, 6144], P('dp'), may hold values from 0 to 1, as said below
- self_in: bfloat16 [768, 3, 768], P(None, None, 'head'), may hold values from -0.21875 to 0.21875
- self_in_bias: float32 [2, 768], P(None, 'head'), may hold values from -3 to 3
- self_out: bfloat16 [768, 768], P('head'), may hold values from -0.625 to 0.625
- cross_in: bfloat16 [768, 3, 768], P(None, None, 'head'), may hold values from -0.21875 to 0.21875
- cross_in_bias: float32 [2, 768], P(None, 'head'), may hold values from -3 to 3
- cross_out: bfloat16 [768, 768], P('head'), may hold values from -0.625 to 0.625
- ffn_up: bfloat16 [768, 3072], P(None, 'head'), may hold values from -0.21875 to 0.21875
- ffn_up_bias: float32 [3072], P('head'), may hold values from -3 to 3
- ffn_down: bfloat16 [3072, 768], P('head'), may hold values from -0.109375 to 0.109375
- out_biases: float32 [3, 768], replicated, may hold values from -3 to 3
- norm_gains: float32 [3, 768], replicated, may hold values from 0.5 to 1.5
- norm_biases: float32 [3, 768], replicated, may hold values from -1.25 to 1.25
- cotangent: bfloat16 [4, 1024, 768], P('dp', 'seq'), may hold values from -6 to 6
Outputs:
- layer_out: float32 [4, 1024, 768], P('dp', 'seq')
- target_grad: float32 [4, 1024, 768], P('dp', 'seq')
- memory_grad: float32 [4, 6144, 768], P('dp', ('seq', 'head'))
- self_in_grad: float32 [768, 3, 768], P('dp', None, 'head')
- self_in_bias_grad: float32 [2, 768], P(None, 'head')
- self_out_grad: float32 [768, 768], P('head', 'dp')
- cross_in_grad: float32 [768, 3, 768], P('dp', None, 'head')
- cross_in_bias_grad: float32 [2, 768], P(None, 'head')
- cross_out_grad: float32 [768, 768], P('head', 'dp')
- ffn_up_grad: float32 [768, 3072], P('dp', 'head')
- ffn_up_bias_grad: float32 [3072], P('head')
- ffn_down_grad: float32 [3072, 768], P('head', 'dp')
- out_biases_grad: float32 [3, 768], replicated
- norm_gains_grad: float32 [3, 768], replicated
- norm_biases_grad: float32 [3, 768], replicated
The draws below stay inside these ranges and needn't reach their ends.
Inputs may be any that keep to these rules, and one draw needn't show every extreme that they name: `memory_mark`: every item has a 1 in each aligned block of 1536 memory rows.
All inputs are finite; a program needn't handle non-finite values.
Results may differ from the reference program's by a relative error of at most 0.025.
The reference program's roundings to bfloat16 on the way count: a program that leaves them out, or rounds other values in their place, can miss the bound.
Values may be sent and summed in bfloat16 or wider, within the bound.
No kernel may reach another device: no remote copies, remote signals or barrier semaphores. Data moves between devices by JAX's collectives and lax.ppermute only.
A program may use at most 128 MiB of HBM per device.

```python
import jax
import jax.numpy as jnp
from jax import lax

D = 768
HEADS = 12
HEAD_DIM = 64
FF = 3072
MEM_DEV = 1536
BATCH = 4
TGT = 1024
MEM = 6144


def draw_memory_mark(key, part):
    key = jax.random.fold_in(key, 11)
    level_key, pick_key, anchor_key = jax.random.split(key, 3)
    blocks = MEM // MEM_DEV
    levels = jax.random.randint(level_key, (BATCH, blocks, 1), 0, 6)
    pick_value = jax.random.randint(pick_key, (BATCH, blocks, MEM_DEV), 0, 32)
    anchor_rows = jax.random.randint(anchor_key, (BATCH, blocks, 1), 0, MEM_DEV)
    places = lax.broadcasted_iota(jnp.int32, (BATCH, blocks, MEM_DEV), 2)
    chosen = (pick_value < jnp.right_shift(32, levels)) | (places == anchor_rows)
    return chosen.astype(jnp.int32).reshape(BATCH, MEM)


def steps_of(key, shape, shards, smallest, largest):
    loudness, own = 1.0, jax.random.fold_in(key, 6)
    for dim, blocks in shards:
        steps = jnp.exp(jax.random.uniform(jax.random.fold_in(own, dim), (blocks,), jnp.float32, smallest / len(shards), largest / len(shards)))
        loudness = loudness * jnp.repeat(steps, shape[dim] // blocks).reshape([-1 if axis == dim else 1 for axis in range(len(shape))])
    return loudness


def noise(rng, shape, deviation, limit, pieces=(), dtype=jnp.bfloat16):
    drawn = deviation * jax.random.normal(rng, shape, jnp.float32)
    if pieces:
        drawn = drawn * steps_of(rng, shape, pieces, -0.22, 0.18)
    return jnp.clip(drawn, -limit, limit).astype(dtype)


def setup_inputs(seed: int = 0) -> dict:
    arg_keys = jax.random.split(jax.random.key(seed), 17)
    target = noise(arg_keys[0], (BATCH, TGT, D), 1.0, 6.0, ((0, 2), (1, 4)))
    memory = noise(arg_keys[1], (BATCH, MEM, D), 1.0, 6.0, ((0, 2), (1, 4)))
    memory_mark = draw_memory_mark(jax.random.fold_in(arg_keys[16], 71), 0)
    self_in = noise(arg_keys[3], (D, 3, D), D ** -0.5, 0.21875, ((2, 4),))
    self_in_bias = noise(arg_keys[4], (2, D), 0.5, 3.0, ((1, 4),), jnp.float32)
    self_out = noise(arg_keys[5], (D, D), (D // 8) ** -0.5, 0.625, ((0, 4),))
    cross_in = noise(arg_keys[6], (D, 3, D), D ** -0.5, 0.21875, ((2, 4),))
    cross_in_bias = noise(arg_keys[7], (2, D), 0.5, 3.0, ((1, 4),), jnp.float32)
    cross_out = noise(arg_keys[8], (D, D), (D // 8) ** -0.5, 0.625, ((0, 4),))
    ffn_up = noise(arg_keys[9], (D, FF), D ** -0.5, 0.21875, ((1, 4),))
    ffn_up_bias = noise(arg_keys[10], (FF,), 0.5, 3.0, ((0, 4),), jnp.float32)
    ffn_down = noise(arg_keys[11], (FF, D), FF ** -0.5, 0.109375, ((0, 4),))
    out_biases = noise(arg_keys[12], (3, D), 0.5, 3.0, (), jnp.float32)
    norm_gains = jnp.clip(1.0 + 0.1 * jax.random.normal(arg_keys[13], (3, D), jnp.float32), 0.5, 1.5)
    norm_biases = noise(arg_keys[14], (3, D), 0.2, 1.25, (), jnp.float32)
    cotangent = noise(arg_keys[15], (BATCH, TGT, D), 1.0, 6.0, ((0, 2), (1, 4)))
    return dict(target=target, memory=memory, memory_mark=memory_mark, self_in=self_in, self_in_bias=self_in_bias, self_out=self_out, cross_in=cross_in, cross_in_bias=cross_in_bias, cross_out=cross_out, ffn_up=ffn_up, ffn_up_bias=ffn_up_bias, ffn_down=ffn_down, out_biases=out_biases, norm_gains=norm_gains, norm_biases=norm_biases, cotangent=cotangent)


exact_mode = lax.Precision.HIGHEST
masked_score = -1e+30
norm_epsilon = 1e-05

@jax.custom_vjp
def low(v):
    return lax.optimization_barrier(v.astype(jnp.bfloat16)).astype(jnp.float32)

@jax.custom_vjp
def low_back(v):
    return v

def low_keep(v):
    return (low(v), None)

def low_pass(kept, grad):
    return (grad,)

def back_keep(v):
    return (v, None)

def back_low(kept, grad):
    return (low(grad),)
low.defvjp(low_keep, low_pass)
low_back.defvjp(back_keep, back_low)

def rounded(matrix):
    return low(low_back(matrix))

def layer_norm(matrix, gain, shift):
    center = matrix - lax.optimization_barrier(jnp.mean(matrix, axis=-1, keepdims=True))
    spread = lax.optimization_barrier(jnp.mean(center * center, axis=-1, keepdims=True))
    return center * lax.rsqrt(spread + norm_epsilon) * gain + shift

def project(matrix, weight):
    return jnp.einsum('btd,dx->btx', matrix, weight, precision=exact_mode)

def split_heads(matrix):
    return jnp.transpose(matrix.reshape(matrix.shape[0], matrix.shape[1], HEADS, HEAD_DIM), (0, 2, 1, 3))

def merge_heads(matrix):
    return jnp.transpose(matrix, (0, 2, 1, 3)).reshape(matrix.shape[0], matrix.shape[2], HEADS * HEAD_DIM)

def softmax_rows(scores):
    biggest = lax.optimization_barrier(jnp.max(scores, axis=-1, keepdims=True))
    scaled = jnp.exp(scores - biggest)
    return scaled / lax.optimization_barrier(jnp.sum(scaled, axis=-1, keepdims=True))

def one_head(queries, key_rows, values, allowed):
    scores = low_back(jnp.dot(queries, key_rows.T, precision=exact_mode))
    scores = jnp.where(allowed, scores, masked_score)
    return jnp.dot(low(softmax_rows(scores)), values, precision=exact_mode)

def causal_head(parts):
    queries, key_rows, values = parts
    extent = (queries.shape[0], key_rows.shape[0])
    allowed = lax.broadcasted_iota(jnp.int32, extent, 0) >= lax.broadcasted_iota(jnp.int32, extent, 1)
    return one_head(queries, key_rows, values, allowed)

def marked_head(parts):
    queries, key_rows, values, marks = parts
    return one_head(queries, key_rows, values, (marks > 0)[None, :])

def causal_item(parts):
    return lax.map(jax.checkpoint(causal_head), parts)

def marked_item(parts):
    queries, key_rows, values, marks = parts
    spread_marks = jnp.broadcast_to(marks, (HEADS, marks.shape[0]))
    return lax.map(jax.checkpoint(marked_head), (queries, key_rows, values, spread_marks))

def forward(target, memory, self_in, self_in_bias, self_out, cross_in, cross_in_bias, cross_out, ffn_up, ffn_up_bias, ffn_down, out_biases, norm_gains, norm_biases, memory_mark):
    query_one = rounded((project(target, self_in[:, 0]) + self_in_bias[0]) * 0.125)
    key_one = rounded(project(target, self_in[:, 1]))
    value_one = rounded(project(target, self_in[:, 2]) + self_in_bias[1])
    attn_one = rounded(merge_heads(lax.map(causal_item, (split_heads(query_one), split_heads(key_one), split_heads(value_one)))))
    sum_one = target + low_back(project(attn_one, self_out) + out_biases[0])
    hidden_one = layer_norm(sum_one, norm_gains[0], norm_biases[0])
    query_two = rounded((project(low(hidden_one), cross_in[:, 0]) + cross_in_bias[0]) * 0.125)
    key_two = rounded(project(memory, cross_in[:, 1]))
    value_two = rounded(project(memory, cross_in[:, 2]) + cross_in_bias[1])
    attn_two = rounded(merge_heads(lax.map(marked_item, (split_heads(query_two), split_heads(key_two), split_heads(value_two), memory_mark))))
    sum_two = hidden_one + low_back(project(attn_two, cross_out) + out_biases[1])
    hidden_two = layer_norm(sum_two, norm_gains[1], norm_biases[1])
    pre_act = low_back(project(low(hidden_two), ffn_up) + ffn_up_bias)
    active = low(jax.nn.gelu(pre_act, approximate=False))
    sum_three = hidden_two + low_back(project(active, ffn_down) + out_biases[2])
    return layer_norm(sum_three, norm_gains[2], norm_biases[2])

def reference(target, memory, memory_mark, self_in, self_in_bias, self_out, cross_in, cross_in_bias, cross_out, ffn_up, ffn_up_bias, ffn_down, out_biases, norm_gains, norm_biases, cotangent):
    floats = tuple((tensor.astype(jnp.float32) for tensor in (target, memory, self_in, self_in_bias, self_out, cross_in, cross_in_bias, cross_out, ffn_up, ffn_up_bias, ffn_down, out_biases, norm_gains, norm_biases)))

    def run_layer(*params):
        return forward(*params, memory_mark)
    result, pullback = jax.vjp(run_layer, *floats)
    gradients = pullback(cotangent.astype(jnp.float32))
    return (result, gradients[0], gradients[1], gradients[2], gradients[3], gradients[4], gradients[5], gradients[6], gradients[7], gradients[8], gradients[9], gradients[10], gradients[11], gradients[12], gradients[13])
```

```python
import jax
import jax.numpy as jnp
from jax import lax
from jax.experimental import pallas as pl
from jax.experimental.pallas import tpu as pltpu
from jax.sharding import PartitionSpec as P

HEAD_DIM = 64
masked_score = -1e30
norm_epsilon = 1e-05
low = jnp.bfloat16
full = jnp.float32
STAT_ROWS = 16
KEY_ROWS = 256


def nn(a, b):
    return lax.dot_general(a, b, (((1,), (0,)), ((), ())), preferred_element_type=full)


def nt(a, b):
    return lax.dot_general(a, b, (((1,), (1,)), ((), ())), preferred_element_type=full)


def tn(a, b):
    return lax.dot_general(a, b, (((0,), (0,)), ((), ())), preferred_element_type=full)


def cells(shape, dtype):
    return jax.ShapeDtypeStruct(shape, dtype)


def flops(count):
    return pl.CostEstimate(flops=int(count), bytes_accessed=4_000_000, transcendentals=0)


def kernel_call(body, name, place, operands, outs, scratch=(), anywhere=(), cost=1e9):
    whole = pl.BlockSpec(memory_space=pltpu.VMEM)
    hbm = pl.BlockSpec(memory_space=pl.ANY)
    specs = [pl.BlockSpec(memory_space=pltpu.SMEM)]
    specs += [hbm if n in anywhere else whole for n in range(len(operands))]
    return pl.pallas_call(
        body,
        name=name,
        in_specs=specs,
        out_specs=[whole] * len(outs),
        out_shape=list(outs),
        scratch_shapes=list(scratch),
        cost_estimate=flops(cost),
        compiler_params=pltpu.CompilerParams(vmem_limit_bytes=58 * 2**20),
    )(place, *operands)


def swap(x, axis, mask):
    size = lax.axis_size(axis)
    return lax.ppermute(x, axis, [(i, i ^ mask) for i in range(size)])


def head_exchange(pieces):
    return [pieces[0]] + [swap(pieces[k], "head", k) for k in range(1, 4)]


def seq_gather(x):
    far = swap(x, "seq", 2)
    return [x, swap(x, "seq", 1), far, swap(far, "seq", 1)]


def seq_exchange(pieces):
    return [pieces[0]] + [swap(pieces[j], "seq", j) for j in range(1, 4)]


def gather_parts(part, stages):
    slots = {0: jnp.stack([part] + [swap(part, "head", k) for k in range(1, 4)])}
    for axis, mask, bit in stages:
        for c in list(slots):
            slots[c | bit] = swap(slots[c], axis, mask)
    return [slots[c] for c in range(len(slots))]


def norm_forward(x, gain, shift):
    center = x - jnp.mean(x, axis=-1, keepdims=True)
    spread = jnp.mean(center * center, axis=-1, keepdims=True)
    scale = lax.rsqrt(spread + norm_epsilon)
    normed = center * scale
    return normed * gain + shift, normed, scale


def norm_backward(grad, normed, scale, gain):
    g = grad * gain
    mean_g = jnp.mean(g, axis=-1, keepdims=True)
    mean_gn = jnp.mean(g * normed, axis=-1, keepdims=True)
    return scale * (g - mean_g - normed * mean_gn)


def column_sum(x):
    return jnp.sum(x, axis=0, keepdims=True)


def two_parts(x):
    high = x.astype(low).astype(full)
    return [high, x - high]


def self_project(place, target, weight, bias, query_t, pair_t):
    rows = target.shape[0] // 2
    width = bias.shape[1]
    row = jnp.concatenate([bias[0:1], jnp.zeros((1, width), full), bias[1:2]], axis=1)
    proj = nn(target[...], weight[...]) + row
    lane = lax.broadcasted_iota(jnp.int32, proj.shape, 1)
    proj = jnp.where(lane < width, proj * 0.125, proj)
    turned = proj.T.astype(low)
    for i in range(2):
        part = turned[:, i * rows : (i + 1) * rows]
        query_t[i] = part[:width]
        pair_t[i] = part[width:]


def self_scores(place, key_t, query, j):
    scores = tn(key_t, query)
    seq_place = place[1]
    if j == 0:
        key_pos = lax.broadcasted_iota(jnp.int32, scores.shape, 0)
        query_pos = lax.broadcasted_iota(jnp.int32, scores.shape, 1)
        return jnp.where(query_pos >= key_pos, scores, masked_score)
    return scores + jnp.where((seq_place ^ j) < seq_place, 0.0, masked_score).astype(full)


def self_forward(place, query_t, p0, p1, p2, p3, a0, a1, a2, a3, attn, logs, held):
    pairs = (p0, p1, p2, p3)
    width = query_t.shape[1]
    for i in range(2):
        rows = []
        for h in range(width // HEAD_DIM):
            at = slice(h * HEAD_DIM, (h + 1) * HEAD_DIM)
            vat = slice(width + h * HEAD_DIM, width + (h + 1) * HEAD_DIM)
            query = query_t[i, at]
            scores = [self_scores(place, pairs[j][i, at], query, j) for j in range(4)]
            top = jnp.max(scores[0], axis=0, keepdims=True)
            for j in range(1, 4):
                top = jnp.maximum(top, jnp.max(scores[j], axis=0, keepdims=True))
            total, out = 0.0, 0.0
            for j in range(4):
                weights = jnp.exp(scores[j] - top)
                total = total + jnp.sum(weights, axis=0, keepdims=True)
                out = out + nn(pairs[j][i, vat], weights.astype(low))
            out = out * (1.0 / total)
            attn[i, at] = out
            out = out.astype(low)
            held[2 * i, at] = out[:, :128]
            held[2 * i + 1, at] = out[:, 128:]
            rows.append(top + jnp.log(total))
        rows.append(jnp.zeros((8 - len(rows), rows[0].shape[1]), full))
        logs[i] = jnp.concatenate(rows, axis=0)
    for k, out in enumerate((a0, a1, a2, a3)):
        out[...] = held[k ^ place[0]]


def self_backward(
    place, query_t, p0, p1, p2, p3, attn, logs, g0, g1, g2, g3, dquery, d0, d1, d2, d3, held
):
    pairs = (p0, p1, p2, p3)
    grads = (d0, d1, d2, d3)
    width = query_t.shape[1]
    for k, piece in enumerate((g0, g1, g2, g3)):
        held[k ^ place[0]] = piece[...]
    for i in range(2):
        for h in range(width // HEAD_DIM):
            at = slice(h * HEAD_DIM, (h + 1) * HEAD_DIM)
            vat = slice(width + h * HEAD_DIM, width + (h + 1) * HEAD_DIM)
            query = query_t[i, at]
            grad = jnp.concatenate([held[2 * i, at], held[2 * i + 1, at]], axis=1)
            dot = jnp.sum(grad.astype(full) * attn[i, at], axis=0, keepdims=True)
            log_total = logs[i, h : h + 1]
            dq = 0.0
            for j in range(4):
                key_t, value_t = pairs[j][i, at], pairs[j][i, vat]
                weights = jnp.exp(self_scores(place, key_t, query, j) - log_total)
                dscores = (weights * (tn(value_t, grad) - dot)).astype(low)
                dq = dq + nn(key_t, dscores)
                grads[j][i, at] = nt(query, dscores).astype(low)
                grads[j][i, vat] = nt(grad, weights.astype(low)).astype(low)
            dquery[i, at] = dq.astype(low) * 0.125


def memory_project(place, memory, weight, bias, marks, pair, pair_t, extra):
    item = pl.program_id(0) ^ (place[0] // 2)
    proj = (nn(memory[0], weight[...]) + bias[...]).astype(low)
    heads = weight.shape[1] // 128
    rows = proj.shape[0]
    turned = proj.T
    first = lax.broadcasted_iota(jnp.int32, (STAT_ROWS, rows), 0) == 0
    for h in range(heads):
        pair[0, h] = proj[:, 128 * h : 128 * h + 128]
        pair_t[0, h, 0:128] = turned[128 * h : 128 * h + 128]
        pair_t[0, h, 128 : 128 + STAT_ROWS] = first.astype(full).astype(low)
    live = jnp.where(item == 0, marks[0:1], marks[1:2])
    bias_row = jnp.where(live > 0, 0.0, masked_score)
    column = jnp.broadcast_to(bias_row, (128, rows)).T
    lane = lax.broadcasted_iota(jnp.int32, (rows, 128), 1)
    extra[0] = jnp.where(lane == 0, column, jnp.where(lane < 3, 1.0, 0.0)).astype(low)


def slot_lanes(refs, at):
    return jnp.concatenate([refs[j][a, at] for j in range(4) for a in range(2)], axis=1)


def cross_forward(pair, extra, pair_t, q0, q1, q2, q3, o0, o1, o2, o3):
    queries, outs = (q0, q1, q2, q3), (o0, o1, o2, o3)
    heads, key_count = pair.shape[1], pair.shape[2]
    steps = key_count // KEY_ROWS
    count = 8 * 128
    first = lax.broadcasted_iota(jnp.int32, (STAT_ROWS, count), 0) == 0
    ones_row = first.astype(full).astype(low)
    stats = []
    for h in range(heads):
        query = slot_lanes(queries, slice(64 * h, 64 * h + 64))
        right = jnp.concatenate(
            [query, jnp.zeros((64, count), low), ones_row, jnp.zeros((112, count), low)], axis=0
        )

        def scores_of(n):
            rows = slice(n * KEY_ROWS, (n + 1) * KEY_ROWS)
            return nn(jnp.concatenate([pair[0, h, rows], extra[0, rows]], axis=1), right)

        top = None
        coming = scores_of(0)
        for n in range(steps):
            scores = coming
            if n + 1 < steps:
                coming = scores_of(n + 1)
            here = jnp.max(scores, axis=0, keepdims=True)
            new_top = here if n == 0 else jnp.maximum(top, here)
            weights = jnp.exp(scores - new_top).astype(low)
            part = nn(pair_t[0, h, 64 : 128 + STAT_ROWS, n * KEY_ROWS : (n + 1) * KEY_ROWS], weights)
            total = part if n == 0 else total * jnp.exp(top - new_top) + part
            top = new_top
        amount = total[64:65]
        out = (total[:64] * (1.0 / amount)).astype(low)
        for j in range(4):
            for a in range(2):
                c = (2 * j + a) * 128
                outs[j][a, 64 * h : 64 * h + 64] = out[:, c : c + 128]
        stats += two_parts(top + jnp.log(amount))
    stats.append(jnp.zeros((STAT_ROWS - len(stats), count), full))
    stats = jnp.concatenate(stats, axis=0).astype(low)
    for j in range(4):
        for a in range(2):
            c = (2 * j + a) * 128
            outs[j][a, 64 * heads : 64 * heads + STAT_ROWS] = stats[:, c : c + 128]


def cross_backward(
    place, pair, extra, pair_t, q0, q1, q2, q3, g0, g1, g2, g3, m0, m1, m2, m3, d0, d1, d2, d3,
    held, dquery, score_right, grad_right, query_right, value_right,
):
    queries, grads, douts = (q0, q1, q2, q3), (g0, g1, g2, g3), (d0, d1, d2, d3)
    heads, key_count = pair.shape[1], pair.shape[2]
    count = 8 * 128
    blocks, block_rows = held.shape[0], held.shape[1]
    none = jnp.zeros((64, count), low)
    pad = jnp.zeros((112, count), low)
    one = jnp.ones((1, count), full)
    rest = jnp.zeros((STAT_ROWS - 3, count), full)
    stats = slot_lanes(grads, slice(64 * heads, 64 * heads + STAT_ROWS)).astype(full)
    for h in range(heads):
        at = slice(64 * h, 64 * h + 64)
        query, grad = slot_lanes(queries, at), slot_lanes(grads, at)
        score_rows = jnp.concatenate([one, stats[4 * h : 4 * h + 2], rest], axis=0).astype(low)
        dot_rows = jnp.concatenate([0.0 * one, stats[4 * h + 2 : 4 * h + 4], rest], axis=0).astype(low)
        score_right[...] = jnp.concatenate([query, none, score_rows, pad], axis=0)
        grad_right[...] = jnp.concatenate([none, grad, dot_rows, pad], axis=0)
        query_right[...] = jnp.concatenate([query, none], axis=0)
        value_right[...] = jnp.concatenate([none, grad], axis=0)
        for n in range(key_count // KEY_ROWS):
            rows = slice(n * KEY_ROWS, (n + 1) * KEY_ROWS)
            left = jnp.concatenate([pair[0, h, rows], extra[0, rows]], axis=1)
            weights = jnp.exp(nn(left, score_right[...]))
            dscores = (weights * nn(left, grad_right[...])).astype(low)
            dpair = nt(weights.astype(low), value_right[...]) + nt(dscores, query_right[...])
            dpair = dpair.astype(low)
            done = 0
            while done < KEY_ROWS:
                start = n * KEY_ROWS + done
                block, inner = start // block_rows, start % block_rows
                size = min(KEY_ROWS - done, block_rows - inner)
                held[block, inner : inner + size, 128 * h : 128 * h + 128] = dpair[done : done + size]
                done += size
            part = nn(pair_t[0, h, 0:64, rows], dscores)
            if n == 0:
                dquery[...] = part
            else:
                dquery[...] += part
        for j in range(4):
            for a in range(2):
                c = (2 * j + a) * 128
                douts[j][a, at] = dquery[:, c : c + 128].astype(low)
    for k, out in enumerate((m0, m1, m2, m3)):
        out[0] = held[k ^ place[0]]


def combine_outputs(place, p0, p1, p2, p3, o0, o1, o2, o3):
    parts = (p0, p1, p2, p3)
    width = p0.shape[1] - STAT_ROWS
    heads = width // HEAD_DIM
    for k, out in enumerate((o0, o1, o2, o3)):
        stats = [part[k, width : width + STAT_ROWS].astype(full) for part in parts]
        rows = []
        for h in range(heads):
            at = slice(64 * h, 64 * h + 64)
            logs = [s[2 * h : 2 * h + 1] + s[2 * h + 1 : 2 * h + 2] for s in stats]
            top = jnp.maximum(jnp.maximum(logs[0], logs[1]), jnp.maximum(logs[2], logs[3]))
            shares = [jnp.exp(value - top) for value in logs]
            amount = shares[0] + shares[1] + shares[2] + shares[3]
            inverse = 1.0 / amount
            total = 0.0
            for j in range(4):
                total = total + parts[j][k, at].astype(full) * (shares[j] * inverse)
            out[at] = total.astype(low)
            rows += two_parts(top + jnp.log(amount))
        rows.append(jnp.zeros((STAT_ROWS - len(rows), rows[0].shape[1]), full))
        out[width : width + STAT_ROWS] = jnp.concatenate(rows, axis=0).astype(low)


def combine_queries(place, p0, p1, p2, p3, o0, o1, o2, o3):
    for k, out in enumerate((o0, o1, o2, o3)):
        total = p0[k].astype(full) + p1[k].astype(full) + p2[k].astype(full) + p3[k].astype(full)
        out[...] = total.astype(low) * 0.125


def assemble(slots, scratch, at, part):
    for c, slot in enumerate(slots):
        for k in range(4):
            scratch[k, part ^ c] = slot[k] if at is None else slot[k, at]


def matrix_of(scratch, k):
    parts = scratch[k]
    return parts.reshape(parts.shape[0] * parts.shape[1], parts.shape[2])


def dense_one(
    place, a0, a1, a2, a3, target, s0, s1, s2, s3, query_bias, biases, gains, shifts,
    hidden, hidden_low, normed, scale, q0, q1, q2, q3, out_w, query_w,
):
    part = (place[2] % 2) * 2 + place[1] % 2
    assemble((s0, s1, s2, s3), out_w, 0, part)
    assemble((s0, s1, s2, s3), query_w, 1, part)
    rows = hidden.shape[0]
    total = 0.0
    for k, piece in enumerate((a0, a1, a2, a3)):
        total = total + tn(piece[...], matrix_of(out_w, k))
    mine = target[pl.ds(pl.multiple_of(place[0] * rows, rows), rows), :].astype(full)
    value, n, r = norm_forward(mine + (total + biases[0:1]), gains[0:1], shifts[0:1])
    hidden[...] = value
    value = value.astype(low)
    hidden_low[...] = value
    normed[...] = n
    scale[...] = jnp.broadcast_to(r, scale.shape)
    for k, out in enumerate((q0, q1, q2, q3)):
        query = (nt(value, matrix_of(query_w, k)) + query_bias[k : k + 1]) * 0.125
        out[...] = query.T.astype(low)


def dense_two(place, *refs):
    outs = refs[0:4]
    hidden, cotangent = refs[4:6]
    cross_slots, up_slots, down_slots = refs[6:10], refs[10:18], refs[18:26]
    up_bias, biases, gains, shifts = refs[26:30]
    layer, grad_hidden = refs[30:32]
    grads = refs[32:36]
    shares = refs[36:40]
    rows_out, sums, up_sums = refs[40:43]
    cross_w, up_w, down_w, pre_held, active_held, pre_grad_held, attn_held, sem = refs[43:]
    rows = hidden.shape[0]
    seq_place, data_place = place[1], place[2] % 2
    eighth = data_place * 4 + seq_place
    copies = []
    for c in range(8):
        copies.append(pltpu.make_async_copy(up_slots[c], up_w.at[:, eighth ^ c], sem.at[c]))
        copies.append(pltpu.make_async_copy(down_slots[c], down_w.at[:, eighth ^ c], sem.at[8 + c]))
    for copy in copies:
        copy.start()
    assemble(cross_slots, cross_w, None, data_place * 2 + seq_place % 2)
    width = outs[0].shape[0] - STAT_ROWS
    quarter = width // 4
    total = 0.0
    for k in range(4):
        total = total + tn(outs[k][0:width], matrix_of(cross_w, k))
        for q in range(4):
            attn_held[k, q] = outs[k][q * quarter : (q + 1) * quarter]
    sum_two = hidden[...] + (total + biases[1:2])
    h2, n2, r2 = norm_forward(sum_two, gains[1:2], shifts[1:2])
    h2_low = h2.astype(low)
    for copy in copies:
        copy.wait()
    out = 0.0
    for k in range(4):
        pre = nn(h2_low, matrix_of(up_w, k)) + up_bias[k : k + 1]
        pre_held[k] = pre
        share = 0.5 * (1.0 + lax.erf(pre * 0.7071067811865476))
        active = (pre * share).astype(low)
        out = out + nn(active, matrix_of(down_w, k))
        turned = active.T
        step = turned.shape[0] // 4
        for q in range(4):
            active_held[k, q] = turned[q * step : (q + 1) * step]
    y, n3, r3 = norm_forward(h2 + (out + biases[2:3]), gains[2:3], shifts[2:3])
    layer[...] = y.astype(low)
    cot = cotangent[pl.ds(pl.multiple_of(place[0] * rows, rows), rows), :].astype(full)
    g3 = norm_backward(cot, n3, r3, gains[2:3])
    g3_low = g3.astype(low)
    grad = 0.0
    for k in range(4):
        pre = pre_held[k]
        share = 0.5 * (1.0 + lax.erf(pre * 0.7071067811865476))
        slope = share + pre * (0.3989422804014327 * jnp.exp(-0.5 * pre * pre))
        dpre = (nt(g3_low, matrix_of(down_w, k)) * slope).astype(low)
        grad = grad + nt(dpre, matrix_of(up_w, k))
        up_sums[k : k + 1] = column_sum(dpre.astype(full))
        turned = dpre.T
        step = turned.shape[0] // 4
        for q in range(4):
            pre_grad_held[k, q] = turned[q * step : (q + 1) * step]
    grad = g3 + grad
    g2 = norm_backward(grad, n2, r2, gains[1:2])
    grad_hidden[...] = g2
    g2_low = g2.astype(low)
    for k in range(4):
        dattn = nt(matrix_of(cross_w, k), g2_low).astype(low)
        grads[k][0:width] = dattn
        product = dattn.astype(full) * outs[k][0:width].astype(full)
        stats = outs[k][width : width + STAT_ROWS].astype(full)
        lines = []
        for h in range(width // HEAD_DIM):
            dot = jnp.sum(product[64 * h : 64 * h + 64], axis=0, keepdims=True)
            lines += [-stats[2 * h : 2 * h + 1], -stats[2 * h + 1 : 2 * h + 2]]
            lines += two_parts(-dot)
        lines.append(jnp.zeros((STAT_ROWS - len(lines), rows), full))
        grads[k][width : width + STAT_ROWS] = jnp.concatenate(lines, axis=0).astype(low)
    half = h2_low.shape[1] // 2
    for n, value in enumerate((h2_low, g3_low, g2_low)):
        rows_out[n, 0] = value[:, :half]
        rows_out[n, 1] = value[:, half:]
    step = active_held.shape[2]
    for j in range(4):
        for k in range(4):
            shares[j][k, 0:step] = active_held[k, seq_place ^ j]
            shares[j][k, step : 2 * step] = pre_grad_held[k, seq_place ^ j]
            shares[j][k, 2 * step : 2 * step + quarter] = attn_held[k, seq_place ^ j]
    sums[...] = jnp.concatenate(
        [
            column_sum(g2_low.astype(full)),
            column_sum(g3_low.astype(full)),
            column_sum(grad * n2),
            column_sum(cot * n3),
            column_sum(grad),
            column_sum(cot),
            jnp.zeros((2, h2.shape[1]), full),
        ],
        axis=0,
    )


def dense_three(
    place, d0, d1, d2, d3, a0, a1, a2, a3, grad_hidden, hidden_low, normed, scale,
    s0, s1, s2, s3, gains,
    grad_sum, g0, g1, g2, g3, x0, x1, x2, x3, rows_out, sums, query_sums,
    out_w, query_w, attn_held, query_held,
):
    part = (place[2] % 2) * 2 + place[1] % 2
    assemble((s0, s1, s2, s3), out_w, 0, part)
    assemble((s0, s1, s2, s3), query_w, 1, part)
    total = grad_hidden[...]
    width = d0.shape[0]
    quarter = width // 4
    ones = jnp.ones((8, d0.shape[1]), low)
    for k, (piece, attn) in enumerate(zip((d0, d1, d2, d3), (a0, a1, a2, a3))):
        value = piece[...]
        total = total + tn(value, matrix_of(query_w, k))
        query_sums[8 * k : 8 * k + 8] = nt(ones, value)
        for q in range(4):
            at = slice(q * quarter, (q + 1) * quarter)
            query_held[k, q] = piece[at]
            attn_held[k, q] = attn[at]
    n = normed[...]
    g = norm_backward(total, n, scale[:, 0:1], gains[0:1])
    grad_sum[...] = g
    g_low = g.astype(low)
    for k, out in enumerate((g0, g1, g2, g3)):
        out[...] = nt(matrix_of(out_w, k), g_low).astype(low)
    half = g_low.shape[1] // 2
    for m, value in enumerate((g_low, hidden_low[...])):
        rows_out[m, 0] = value[:, :half]
        rows_out[m, 1] = value[:, half:]
    for j, out in enumerate((x0, x1, x2, x3)):
        for k in range(4):
            out[k, 0:quarter] = attn_held[k, place[1] ^ j]
            out[k, quarter : 2 * quarter] = query_held[k, place[1] ^ j]
    sums[...] = jnp.concatenate(
        [
            column_sum(g_low.astype(full)),
            column_sum(total * n),
            column_sum(total),
            jnp.zeros((5, n.shape[1]), full),
        ],
        axis=0,
    )


def weight_grads(groups):
    def body(place, x0, x1, x2, x3, r0, r1, r2, r3, out):
        shares, rows = (x0, x1, x2, x3), (r0, r1, r2, r3)
        for n, (begin, end) in enumerate(groups):
            for half in range(2):
                right = jnp.concatenate([row[n, half] for row in rows], axis=0)
                for k in range(4):
                    left = jnp.concatenate([share[k, begin:end] for share in shares], axis=1)
                    out[half, k, begin:end] = nn(left, right).astype(low)

    return body


def memory_weight_grad(place, memory, m0, m1, m2, m3, out, sums, total):
    step = pl.program_id(0)
    width = m0.shape[2]
    lines = 0.0
    product = 0.0
    ones = jnp.ones((8, m0.shape[1]), low)
    for k, piece in enumerate((m0, m1, m2, m3)):
        value = piece[0]
        product = product + tn(value, memory[0, k ^ place[0]])
        lines = lines + nn(ones, value)

    @pl.when(step == 0)
    def _():
        total[...] = product
        sums[...] = lines

    @pl.when(step == 1)
    def _():
        sums[...] += lines
        whole = (total[...] + product).astype(low)
        quarter = width // 4
        half = whole.shape[1] // 2
        for q in range(4):
            for n in range(2):
                out[q, n] = whole[q * quarter : (q + 1) * quarter, n * half : (n + 1) * half]


def memory_gradient(place, m0, m1, m2, m3, s0, s1, s2, s3, s4, s5, s6, s7, out, weight):
    eighth = (place[2] % 2) * 4 + place[1]
    assemble((s0, s1, s2, s3, s4, s5, s6, s7), weight, None, eighth)
    for i in range(2):
        total = 0.0
        for k, piece in enumerate((m0, m1, m2, m3)):
            total = total + nn(piece[i], matrix_of(weight, k))
        out[i] = total


def target_partial(place, dquery, dpair, target, weight, o0, o1, o2, o3, grads, sums, held):
    width = dquery.shape[1]
    total = 0.0
    ones = jnp.ones((8, dquery.shape[2]), low)
    lines = 0.0
    for i in range(2):
        turned = jnp.concatenate([dquery[i], dpair[i]], axis=0)
        natural = turned.T
        part = nt(natural, weight[...]).astype(low)
        held[2 * i] = part[:128]
        held[2 * i + 1] = part[128:]
        rows = dquery.shape[2]
        total = total + nn(turned, target[i * rows : (i + 1) * rows])
        lines = lines + nt(ones, turned)
    sums[...] = lines
    total = total.astype(low)
    quarter = total.shape[0] // 4
    half = total.shape[1] // 2
    for q in range(4):
        for n in range(2):
            grads[q, n] = total[q * quarter : (q + 1) * quarter, n * half : (n + 1) * half]
    for k, out in enumerate((o0, o1, o2, o3)):
        out[...] = held[k ^ place[0]]


def add_parts(place, grad, p0, p1, p2, p3, out):
    total = grad[...]
    for part in (p0, p1, p2, p3):
        total = total + part[...].astype(full)
    out[...] = total.astype(low)


def place_rows(place, b0, b1, b2, b3, out):
    rows = b0.shape[0]
    for k, block in enumerate((b0, b1, b2, b3)):
        at = pl.ds(pl.multiple_of((k ^ place[0]) * rows, rows), rows)
        out[at, :] = block[...].astype(full)


def data_total(x):
    size = lax.axis_size("dp")
    place = lax.axis_index("dp")
    if size == 2:
        sent = lax.dynamic_index_in_dim(x, 1 - place, 0, False)
        kept = lax.dynamic_index_in_dim(x, place, 0, False)
        return kept.astype(full) + swap(sent, "dp", 1).astype(full)
    joined = jnp.concatenate([x[0], x[1]], axis=-1).astype(full)
    return lax.psum_scatter(joined, "dp", scatter_dimension=joined.ndim - 1, tiled=True)


def head_total(x, place):
    pieces = head_exchange([x[k] for k in range(4)])
    return sum(piece.astype(full) for piece in pieces)


def ordered(slots, place):
    stacked = jnp.stack(slots)
    return jnp.stack(
        [lax.dynamic_index_in_dim(stacked, q ^ place, 0, False) for q in range(4)]
    )


def seq_reduce_own(grads, seq_place):
    pieces = [
        lax.dynamic_index_in_dim(grads, seq_place ^ j, 0, False) for j in range(4)
    ]
    received = seq_exchange(pieces)
    return sum(piece.astype(full) for piece in received).astype(low)


def shards(
    target, memory, memory_mark, self_in, self_in_bias, self_out, cross_in, cross_in_bias,
    cross_out, ffn_up, ffn_up_bias, ffn_down, out_biases, norm_gains, norm_biases, cotangent,
):
    items, rows, model = target.shape
    width = self_in.shape[2]
    heads = width // HEAD_DIM
    hidden_units = ffn_up.shape[1]
    memory_rows = memory.shape[1]
    tokens = items * rows
    block = tokens // 4
    head_place = lax.axis_index("head")
    seq_place = lax.axis_index("seq")
    data_place = lax.axis_index("dp")
    place = jnp.stack([head_place, seq_place, data_place]).astype(jnp.int32)
    near = (data_place % 2) * 2 + seq_place % 2
    eighth = (data_place % 2) * 4 + seq_place
    flat_target = target.reshape(tokens, model)
    flat_cotangent = cotangent.reshape(tokens, model)

    self_weight = self_in.reshape(model, 3 * width)
    query_t, pair_t = kernel_call(
        self_project, "self_project", place, (flat_target, self_weight, self_in_bias),
        (cells((items, width, rows), low), cells((items, 2 * width, rows), low)),
    )
    pairs = seq_gather(pair_t)

    cross_query_t = cross_in[:, 0].T
    early = jnp.stack([self_out, cross_query_t])
    quarter = width // 4
    early = lax.dynamic_slice_in_dim(early, near * quarter, quarter, 1)
    near_stages = (("dp", 1, 2), ("seq", 1, 1))
    early_slots = gather_parts(early, near_stages)
    bias_row = jnp.concatenate(
        [ffn_up_bias, cross_in_bias[0], jnp.zeros((256 - width,), full)]
    ).reshape(8, -1)
    bias_rows = jnp.stack([bias_row] + [swap(bias_row, "head", k) for k in range(1, 4)])
    bias_rows = bias_rows.reshape(4, -1)
    up_bias, query_bias = bias_rows[:, :hidden_units], bias_rows[:, hidden_units : hidden_units + width]
    cross_slots = gather_parts(
        lax.dynamic_slice_in_dim(cross_out, near * quarter, quarter, 0), near_stages
    )
    step = model // 8
    up_slots = gather_parts(
        lax.dynamic_slice_in_dim(ffn_up, eighth * step, step, 0),
        (("dp", 1, 4), ("seq", 2, 2), ("seq", 1, 1)),
    )
    step = hidden_units // 8
    down_slots = gather_parts(
        lax.dynamic_slice_in_dim(ffn_down, eighth * step, step, 0),
        (("seq", 2, 2), ("dp", 1, 4), ("seq", 1, 1)),
    )

    pair_weight = cross_in[:, 1:].reshape(model, 2, heads, HEAD_DIM)
    pair_weight = jnp.transpose(pair_weight, (0, 2, 1, 3)).reshape(model, 2 * width)
    value_bias = cross_in_bias[1].reshape(heads, 1, HEAD_DIM)
    pair_bias = jnp.concatenate([jnp.zeros_like(value_bias), value_bias], axis=1).reshape(1, 2 * width)
    step = 2 * width // 8
    pair_slots = gather_parts(
        lax.dynamic_slice_in_dim(pair_weight.T, eighth * step, step, 0),
        (("dp", 1, 4), ("seq", 2, 2), ("seq", 1, 1)),
    )
    row_step = 512
    row_steps = memory_rows // row_step
    memory_pair, memory_pair_t, memory_extra = pl.pallas_call(
        memory_project,
        name="memory_project",
        grid_spec=pltpu.PrefetchScalarGridSpec(
            num_scalar_prefetch=1,
            grid=(items, row_steps),
            in_specs=[
                pl.BlockSpec((1, row_step, model), lambda i, r, p: (i ^ (p[0] // 2), r, 0)),
                pl.BlockSpec((model, 2 * width), lambda i, r, p: (0, 0)),
                pl.BlockSpec((1, 2 * width), lambda i, r, p: (0, 0)),
                pl.BlockSpec((items, row_step), lambda i, r, p: (0, p[1] * row_steps + r)),
            ],
            out_specs=[
                pl.BlockSpec((1, heads, row_step, 128), lambda i, r, p: (i, 0, r, 0)),
                pl.BlockSpec((1, heads, 128 + STAT_ROWS, row_step), lambda i, r, p: (i, 0, 0, r)),
                pl.BlockSpec((1, row_step, 128), lambda i, r, p: (i, r, 0)),
            ],
        ),
        out_shape=[
            cells((items, heads, memory_rows, 128), low),
            cells((items, heads, 128 + STAT_ROWS, memory_rows), low),
            cells((items, memory_rows, 128), low),
        ],
        cost_estimate=flops(4e9),
        compiler_params=pltpu.CompilerParams(vmem_limit_bytes=58 * 2**20),
    )(place, memory, pair_weight, pair_bias, memory_mark)

    piece = cells((width, block), low)
    attn_pieces = kernel_call(
        self_forward, "self_forward", place, (query_t, *pairs),
        [piece] * 4 + [cells((items, width, rows), full), cells((items, 8, rows), full)],
        scratch=[pltpu.VMEM((4, width, block), low)],
    )
    attn_one, logs_one = attn_pieces[4:]
    attn_pieces = head_exchange(attn_pieces[:4])

    near_matrix = pltpu.VMEM((4, 4, quarter, model), low)
    token_rows, token_rows_low = cells((block, model), full), cells((block, model), low)
    hidden_one, hidden_one_low, normed_one, scale_one, *queries = kernel_call(
        dense_one, "dense_one", place,
        (*attn_pieces, flat_target, *early_slots, query_bias, out_biases, norm_gains, norm_biases),
        [token_rows, token_rows_low, token_rows, cells((block, 128), full)] + [piece] * 4,
        scratch=[near_matrix, near_matrix],
    )
    queries = seq_gather(jnp.stack(head_exchange(queries)))

    pair_specs = [
        pl.BlockSpec((1, heads, memory_rows, 128), lambda i, *p: (i, 0, 0, 0)),
        pl.BlockSpec((1, memory_rows, 128), lambda i, *p: (i, 0, 0)),
        pl.BlockSpec((1, heads, 128 + STAT_ROWS, memory_rows), lambda i, *p: (i, 0, 0, 0)),
    ]
    slot = pl.BlockSpec((2, width, block), lambda i, *p: (i, 0, 0))
    stat_slot = pl.BlockSpec((2, width + STAT_ROWS, block), lambda i, *p: (i, 0, 0))
    outs = pl.pallas_call(
        cross_forward,
        name="cross_forward",
        grid=(items,),
        in_specs=pair_specs + [slot] * 4,
        out_specs=[stat_slot] * 4,
        out_shape=[cells((4, width + STAT_ROWS, block), low)] * 4,
        cost_estimate=flops(15e9),
        compiler_params=pltpu.CompilerParams(vmem_limit_bytes=58 * 2**20),
    )(memory_pair, memory_extra, memory_pair_t, *queries)
    stat_piece = cells((width + STAT_ROWS, block), low)
    outs = kernel_call(
        combine_outputs, "combine_outputs", place, seq_exchange(outs), [stat_piece] * 4
    )
    outs = head_exchange(outs)

    share_rows = 2 * (hidden_units // 4) + quarter
    half = model // 2
    dense = kernel_call(
        dense_two, "dense_two", place,
        (*outs, hidden_one, flat_cotangent, *cross_slots, *up_slots, *down_slots,
         up_bias, out_biases, norm_gains, norm_biases),
        [token_rows_low, token_rows] + [stat_piece] * 4
        + [cells((4, share_rows, block), low)] * 4
        + [cells((3, 2, block, half), low), cells((8, model), full), cells((4, hidden_units), full)],
        scratch=[
            near_matrix,
            pltpu.VMEM((4, 8, model // 8, hidden_units), low),
            pltpu.VMEM((4, 8, hidden_units // 8, model), low),
            pltpu.VMEM((4, block, hidden_units), full),
            pltpu.VMEM((4, 4, hidden_units // 4, block), low),
            pltpu.VMEM((4, 4, hidden_units // 4, block), low),
            pltpu.VMEM((4, 4, quarter, block), low),
            pltpu.SemaphoreType.DMA((16,)),
        ],
        anywhere=range(10, 26),
        cost=3e9,
    )
    layer_block, grad_hidden = dense[0:2]
    grads = seq_gather(jnp.stack(head_exchange(dense[2:6])))
    shares, row_pack, sums_mid, up_sums = dense[6:10], dense[10], dense[11], dense[12]

    memory_block = memory_rows // 4
    back = pl.pallas_call(
        cross_backward,
        name="cross_backward",
        grid_spec=pltpu.PrefetchScalarGridSpec(
            num_scalar_prefetch=1,
            grid=(items,),
            in_specs=pair_specs + [slot] * 4 + [stat_slot] * 4,
            out_specs=[
                pl.BlockSpec((1, memory_block, 2 * width), lambda i, p: (i ^ (p[0] // 2), 0, 0))
            ] * 4 + [slot] * 4,
            scratch_shapes=[
                pltpu.VMEM((4, memory_block, 2 * width), low),
                pltpu.VMEM((64, 1024), full),
                pltpu.VMEM((256, 1024), low),
                pltpu.VMEM((256, 1024), low),
                pltpu.VMEM((128, 1024), low),
                pltpu.VMEM((128, 1024), low),
            ],
        ),
        out_shape=[cells((items, memory_block, 2 * width), low)] * 4
        + [cells((4, width, block), low)] * 4,
        cost_estimate=flops(30e9),
        compiler_params=pltpu.CompilerParams(vmem_limit_bytes=58 * 2**20),
    )(place, memory_pair, memory_extra, memory_pair_t, *queries, *grads)
    memory_pieces, dqueries = back[:4], back[4:]
    dqueries = kernel_call(
        combine_queries, "combine_queries", place, seq_exchange(dqueries), [piece] * 4
    )
    dqueries = head_exchange(dqueries)

    late = kernel_call(
        dense_three, "dense_three", place,
        (*dqueries, *attn_pieces, grad_hidden, hidden_one_low, normed_one, scale_one,
         *early_slots, norm_gains),
        [token_rows] + [piece] * 4 + [cells((4, 2 * quarter, block), low)] * 4
        + [cells((2, 2, block, half), low), cells((8, model), full), cells((32, width), full)],
        scratch=[near_matrix, near_matrix]
        + [pltpu.VMEM((4, 4, quarter, block), low)] * 2,
    )
    grad_sum_one = late[0]
    grads_one = head_exchange(late[1:5])
    shares_late, row_pack_late, sums_late, query_sums = late[5:9], late[9], late[10], late[11]

    pair_cells = cells((items, 2 * width, rows), low)
    dquery, *dpairs = kernel_call(
        self_backward, "self_backward", place,
        (query_t, *pairs, attn_one, logs_one, *grads_one),
        [cells((items, width, rows), low)] + [pair_cells] * 4,
        scratch=[pltpu.VMEM((4, width, block), low)],
    )
    kept = dpairs[0].astype(full) + swap(dpairs[1], "seq", 1).astype(full)
    sent = dpairs[2].astype(full) + swap(dpairs[3], "seq", 1).astype(full)
    dpair = (kept + swap(sent.astype(low), "seq", 2).astype(full)).astype(low)

    last = kernel_call(
        target_partial, "target_partial", place, (dquery, dpair, flat_target, self_weight),
        [token_rows_low] * 4
        + [cells((4, 2, 3 * width // 4, half), low), cells((8, 3 * width), full)],
        scratch=[pltpu.VMEM((4, block, model), low)],
    )
    target_block = kernel_call(
        add_parts, "add_parts", place, (grad_sum_one, *head_exchange(last[:4])), [token_rows_low]
    )[0]

    def all_rows(part, name):
        blocks = [part] + [swap(part, "head", k) for k in range(1, 4)]
        out = kernel_call(place_rows, name, place, blocks, [cells((tokens, model), full)])[0]
        return out.reshape(items, rows, model)

    layer_out = all_rows(layer_block, "layer_rows")
    target_grad = all_rows(target_block, "target_rows")

    received = head_exchange(memory_pieces)
    memory_grad = kernel_call(
        memory_gradient, "memory_gradient", place, (*received, *pair_slots),
        [cells((items, memory_block, model), full)],
        scratch=[pltpu.VMEM((4, 8, 2 * width // 8, model), low)],
    )[0]

    def token_weights(shares, pack, groups, name):
        parts = kernel_call(
            weight_grads(groups), name, place, (*seq_exchange(shares), *seq_gather(pack)),
            [cells((2, 4, groups[-1][1], half), low)],
        )[0]
        mine = head_total(data_total(parts).astype(low), head_place).astype(low)
        return ordered(seq_gather(mine), seq_place)

    unit_step = hidden_units // 4
    mid = token_weights(
        shares, row_pack,
        ((unit_step, 2 * unit_step), (0, unit_step), (2 * unit_step, share_rows)), "weights_mid",
    )
    ffn_down_grad = mid[:, 0:unit_step].reshape(hidden_units, -1).astype(full)
    ffn_up_grad = mid[:, unit_step : 2 * unit_step].reshape(hidden_units, -1).T.astype(full)
    cross_out_grad = mid[:, 2 * unit_step :].reshape(width, -1).astype(full)
    end = token_weights(
        shares_late, row_pack_late, ((0, quarter), (quarter, 2 * quarter)), "weights_late"
    )
    self_out_grad = end[:, 0:quarter].reshape(width, -1).astype(full)
    cross_query_grad = end[:, quarter:].reshape(width, -1)

    memory_parts, memory_sums = pl.pallas_call(
        memory_weight_grad,
        name="memory_weight_grad",
        grid_spec=pltpu.PrefetchScalarGridSpec(
            num_scalar_prefetch=1,
            grid=(items,),
            in_specs=[pl.BlockSpec((1, 4, memory_block, model), lambda i, p: (i, 0, 0, 0))]
            + [pl.BlockSpec((1, memory_block, 2 * width), lambda i, p: (i, 0, 0))] * 4,
            out_specs=[
                pl.BlockSpec((4, 2, width // 2, half), lambda i, p: (0, 0, 0, 0)),
                pl.BlockSpec((8, 2 * width), lambda i, p: (0, 0)),
            ],
            scratch_shapes=[pltpu.VMEM((2 * width, model), full)],
        ),
        out_shape=[cells((4, 2, width // 2, half), low), cells((8, 2 * width), full)],
        cost_estimate=flops(2e9),
        compiler_params=pltpu.CompilerParams(vmem_limit_bytes=58 * 2**20),
    )(place, memory.reshape(items, 4, memory_block, model), *memory_pieces)

    def own_weights(grads):
        mine = data_total(seq_reduce_own(grads, seq_place)).astype(low)
        whole = ordered(seq_gather(mine), seq_place)
        return whole.reshape(-1, whole.shape[2])

    self_in_grad = own_weights(last[4])
    share = self_in_grad.shape[1]
    self_in_grad = self_in_grad.T.reshape(share, 3, width).astype(full)
    pair_grad = own_weights(memory_parts).T.reshape(share, heads, 2, HEAD_DIM)
    pair_grad = jnp.transpose(pair_grad, (0, 2, 1, 3)).reshape(share, 2, width)
    cross_in_grad = jnp.concatenate([cross_query_grad.T[:, None], pair_grad], axis=1).astype(full)

    up_own = up_sums
    query_own = query_sums.reshape(4, 8, width)[:, 0]
    by_head = jnp.concatenate([up_own, query_own], axis=1)
    by_head = jnp.stack(
        [lax.dynamic_index_in_dim(by_head, t ^ head_place, 0, False) for t in range(4)]
    )
    value_sums = memory_sums[0].reshape(heads, 2, HEAD_DIM)[:, 1].reshape(width)
    own_sums = jnp.concatenate([last[5][0, :width], last[5][0, 2 * width :], value_sums])
    sums_all, by_head = lax.psum(
        (jnp.concatenate([sums_late[0:3], sums_mid[0:6]]), by_head), ("dp", "seq", "head")
    )
    own_sums = lax.psum(own_sums, ("dp", "seq"))
    mine = lax.dynamic_index_in_dim(by_head, head_place, 0, False)
    self_bias_grad = own_sums[: 2 * width].reshape(2, width)
    cross_bias_grad = jnp.stack([mine[hidden_units:], own_sums[2 * width :]])
    out_bias_grad = jnp.stack([sums_all[0], sums_all[3], sums_all[4]])
    gain_grad = jnp.stack([sums_all[1], sums_all[5], sums_all[6]])
    shift_grad = jnp.stack([sums_all[2], sums_all[7], sums_all[8]])
    return (
        layer_out,
        target_grad,
        memory_grad,
        self_in_grad,
        self_bias_grad,
        self_out_grad,
        cross_in_grad,
        cross_bias_grad,
        cross_out_grad,
        ffn_up_grad,
        mine[:hidden_units],
        ffn_down_grad,
        out_bias_grad,
        gain_grad,
        shift_grad,
    )


def solution(mesh):
    return jax.shard_map(
        shards,
        mesh=mesh,
        in_specs=(
            P("dp", "seq", None),
            P("dp", "seq", None),
            P("dp", None),
            P(None, None, "head"),
            P(None, "head"),
            P("head", None),
            P(None, None, "head"),
            P(None, "head"),
            P("head", None),
            P(None, "head"),
            P("head"),
            P("head", None),
            P(),
            P(),
            P(),
            P("dp", "seq", None),
        ),
        out_specs=(
            P("dp", "seq", None),
            P("dp", "seq", None),
            P("dp", ("seq", "head"), None),
            P("dp", None, "head"),
            P(None, "head"),
            P("head", "dp"),
            P("dp", None, "head"),
            P(None, "head"),
            P("head", "dp"),
            P("dp", "head"),
            P("head"),
            P("head", "dp"),
            P(),
            P(),
            P(),
        ),
        check_vma=False,
    )
```
